32 devices in a mesh: dp: 4 (over z), ctx: 4 (over y, core), tensor: 2 (over x).
Axes of the slice: x: 2, y: 2, z: 4, core: 2. Of those that a mesh axis runs over, the one named last changes fastest.
Arguments:
- tokens: bfloat16 [4096, 4, 2048], P('ctx', 'dp'), may hold values from -6 to 6
- q_weight: bfloat16 [2048, 2048], P(None, 'tensor'), may hold values from -0.125 to 0.125
- k_weight: bfloat16 [2048, 2048], P(None, 'tensor'), may hold values from -0.125 to 0.125
- v_weight: bfloat16 [2048, 2048], P(None, 'tensor'), may hold values from -0.125 to 0.125
- o_weight: bfloat16 [2048, 2048], P(None, 'tensor'), may hold values from -0.125 to 0.125
- gate_weight: bfloat16 [2048, 8192], P(None, 'tensor'), may hold values from -0.125 to 0.125
- up_weight: bfloat16 [2048, 8192], P(None, 'tensor'), may hold values from -0.125 to 0.125
- down_weight: bfloat16 [2048, 8192], P(None, 'tensor'), may hold values from -0.0625 to 0.0625
- q_gain: float32 [2048], P('tensor'), may hold values from 0.3 to 4.5
- k_gain: float32 [2048], P('tensor'), may hold values from 0.3 to 4.5
- attn_gain: float32 [2048], replicated, may hold values from 0.5 to 1.5
- mlp_gain: float32 [2048], replicated, may hold values from 0.5 to 1.5
- group_order: int32 [4, 8], P('dp'), may hold values from 0 to 7, each once within a row
- cotangent: bfloat16 [4096, 4, 2048], P('ctx', 'dp'), may hold values from -6 to 6
Outputs:
- output: bfloat16 [4096, 4, 2048], P('ctx', 'dp')
- input_grad: bfloat16 [4096, 4, 2048], P('ctx', 'dp')
- q_weight_grad: float32 [2048, 2048], P(('dp', 'ctx'), 'tensor')
- k_weight_grad: float32 [2048, 2048], P(('dp', 'ctx'), 'tensor')
- v_weight_grad: float32 [2048, 2048], P(('dp', 'ctx'), 'tensor')
- o_weight_grad: float32 [2048, 2048], P(('dp', 'ctx'), 'tensor')
- gate_weight_grad: float32 [2048, 8192], P(('dp', 'ctx'), 'tensor')
- up_weight_grad: float32 [2048, 8192], P(('dp', 'ctx'), 'tensor')
- down_weight_grad: float32 [2048, 8192], P(('dp', 'ctx'), 'tensor')
- q_gain_grad: float32 [2048], P('tensor')
- k_gain_grad: float32 [2048], P('tensor')
- attn_gain_grad: float32 [2048], replicated
- mlp_gain_grad: float32 [2048], replicated
The draws below stay inside these ranges and needn't reach their ends.
Inputs may be any that keep to these rules, and one draw needn't show every extreme that they name: `group_order`: each row is a permutation of the 8 block numbers.
All inputs are finite; a program needn't handle non-finite values.
Results may differ from the reference program's by a relative error of at most 0.025.
Values may be sent and summed in bfloat16 or wider, within the bound.
No kernel may reach another device: no remote copies, remote signals or barrier semaphores. Data moves between devices by JAX's collectives and lax.ppermute only.
A program may use at most 576 MiB of HBM per device.

```python
import jax
import jax.numpy as jnp
from jax import lax

D = 2048
H = 16
HD = 128
FF = 8192
LEN = 4096
SEQS = 4
GROUPS = 8


def ramp_gain(key, start, finish, rising):
    count = H * HD
    place = jnp.arange(count, dtype=jnp.float32) / (count - 1)
    if not rising:
        place = 1.0 - place
    base = start * jnp.power(finish / start, place)
    jitter = jax.random.uniform(key, (count,), jnp.float32, 0.8, 1.2)
    return (base * jitter).astype(jnp.float32)


def draw_q_gain(key, part):
    key = jax.random.fold_in(key, 11)
    return ramp_gain(key, 0.5, 1.8, True)


def draw_k_gain(key, part):
    key = jax.random.fold_in(key, 23)
    return ramp_gain(key, 0.5, 1.8, False)


def steps_of(own_key, shape, pieces, smallest, high):
    def one(position, shards_of):
        draws = jax.random.uniform(jax.random.fold_in(jax.random.fold_in(own_key, 6), position), (shards_of,), jnp.float32, smallest / len(pieces), high / len(pieces))
        return jnp.repeat(jnp.exp(draws), shape[position] // shards_of).reshape((-1,) + (1,) * (len(shape) - position - 1))

    level = one(*pieces[0])
    for cut in pieces[1:]:
        level = level * one(*cut)
    return level


def gaussian(key, extent, scale, bound, pieces=(), kind=jnp.bfloat16):
    level = steps_of(key, extent, pieces, -0.22, 0.18) if pieces else 1.0
    values = jax.random.normal(key, extent, jnp.float32) * scale * level
    return jnp.minimum(jnp.maximum(values, -bound), bound).astype(kind)


def setup_inputs(seed: int = 0) -> dict:
    arg_keys = jax.random.split(jax.random.key(seed), 15)
    return {
        "tokens": gaussian(arg_keys[0], (LEN, SEQS, D), 1.0, 6.0, ((0, 4), (1, 4))),
        "q_weight": gaussian(arg_keys[1], (D, H * HD), D ** -0.5, 0.125, ((1, 2),)),
        "k_weight": gaussian(arg_keys[2], (D, H * HD), D ** -0.5, 0.125, ((1, 2),)),
        "v_weight": gaussian(arg_keys[3], (D, H * HD), D ** -0.5, 0.125, ((1, 2),)),
        "o_weight": gaussian(arg_keys[4], (D, H * HD), (H * HD) ** -0.5, 0.125, ((1, 2),)),
        "gate_weight": gaussian(arg_keys[5], (D, FF), D ** -0.5, 0.125, ((1, 2),)),
        "up_weight": gaussian(arg_keys[6], (D, FF), D ** -0.5, 0.125, ((1, 2),)),
        "down_weight": gaussian(arg_keys[7], (D, FF), FF ** -0.5, 0.0625, ((1, 2),)),
        "q_gain": draw_q_gain(jax.random.fold_in(arg_keys[14], 71), 0),
        "k_gain": draw_k_gain(jax.random.fold_in(arg_keys[14], 71), 0),
        "attn_gain": jnp.clip(jax.random.uniform(arg_keys[10], (D,), jnp.float32, 0.5, 1.5), 0.5, 1.5),
        "mlp_gain": jnp.clip(jax.random.uniform(arg_keys[11], (D,), jnp.float32, 0.5, 1.5), 0.5, 1.5),
        "group_order": jax.vmap(lambda own: jax.random.permutation(own, GROUPS))(jax.random.split(arg_keys[12], SEQS)).reshape((SEQS, GROUPS)).astype(jnp.int32),
        "cotangent": gaussian(arg_keys[13], (LEN, SEQS, D), 1.0, 6.0, ((0, 4), (1, 4))),
    }


EPS = 1e-06
THETA = 500000.0
BLOCK = 512
HIGH = lax.Precision.HIGHEST

@jax.custom_vjp
def low(v):
    return lax.optimization_barrier(v.astype(jnp.bfloat16)).astype(jnp.float32)

@jax.custom_vjp
def low_back(v):
    return v

def low_keep(v):
    return (low(v), None)

def low_pass(kept, grad):
    return (grad,)

def back_keep(v):
    return (v, None)

def back_low(kept, grad):
    return (low(grad),)
low.defvjp(low_keep, low_pass)
low_back.defvjp(back_keep, back_low)

def rounded_both(value):
    return low_back(low(value))

def matmul(left, right):
    return jnp.dot(left, right, precision=HIGH)

def rms_scale(value):
    return lax.rsqrt(lax.optimization_barrier(jnp.mean(value * value, axis=-1, keepdims=True)) + EPS)

def rotate(value, cosine, sine):
    half = value.shape[-1] // 2
    first = value[..., :half]
    second = value[..., half:]
    return jnp.concatenate([first * cosine - second * sine, second * cosine + first * sine], axis=-1)

def attention(query, keys, values, positions):
    size = min(BLOCK, LEN)
    blocks = LEN // size
    query_blocks = query.reshape(blocks, size, H, HD)
    place_blocks = positions.reshape(blocks, size)
    scale = HD ** (-0.5)

    def one_block(items):
        part, where = items
        scores = jnp.einsum('qhd,khd->hqk', part, keys, precision=HIGH) * scale
        scores = low_back(scores)
        allowed = positions[None, None, :] <= where[None, :, None]
        scores = jnp.where(allowed, scores, -1e+30)
        top = lax.optimization_barrier(jnp.max(scores, axis=-1, keepdims=True))
        expo = jnp.exp(scores - top)
        probs = expo / lax.optimization_barrier(jnp.sum(expo, axis=-1, keepdims=True))
        return jnp.einsum('hqk,khd->qhd', low(probs), values, precision=HIGH)
    result = lax.map(jax.checkpoint(one_block), (query_blocks, place_blocks))
    return result.reshape(LEN, H, HD)

def sequence_layer(params, inputs, positions):
    q_weight, k_weight, v_weight, o_weight, gate_weight, up_weight, down_weight, q_gain, k_gain, attn_gain, mlp_gain = params
    query = low_back(matmul(inputs, q_weight))
    keys = low_back(matmul(inputs, k_weight))
    values = rounded_both(matmul(inputs, v_weight))
    query = query * rms_scale(query) * q_gain
    keys = keys * rms_scale(keys) * k_gain
    freq = jnp.power(THETA, -jnp.arange(HD // 2, dtype=jnp.float32) * 2.0 / HD)
    angle = positions.astype(jnp.float32)[:, None] * freq[None, :]
    cosine = jnp.cos(angle)[:, None, :]
    sine = jnp.sin(angle)[:, None, :]
    query = rounded_both(rotate(query.reshape(LEN, H, HD), cosine, sine))
    keys = rounded_both(rotate(keys.reshape(LEN, H, HD), cosine, sine))
    values = values.reshape(LEN, H, HD)
    attended = attention(query, keys, values, positions)
    attended = rounded_both(attended.reshape(LEN, H * HD))
    branch = low_back(matmul(attended, o_weight.T))
    hidden = inputs + branch * rms_scale(branch) * attn_gain
    lowered = low(hidden)
    gate = low_back(matmul(lowered, gate_weight))
    up = low_back(matmul(lowered, up_weight))
    inner = low(jax.nn.silu(gate) * up)
    mixed = low_back(matmul(inner, down_weight.T))
    return hidden + mixed * rms_scale(mixed) * mlp_gain

def reference(tokens, q_weight, k_weight, v_weight, o_weight, gate_weight, up_weight, down_weight, q_gain, k_gain, attn_gain, mlp_gain, group_order, cotangent):
    params = tuple((w.astype(jnp.float32) for w in (q_weight, k_weight, v_weight, o_weight, gate_weight, up_weight, down_weight, q_gain, k_gain, attn_gain, mlp_gain)))
    block = LEN // GROUPS
    slots = jnp.arange(LEN, dtype=jnp.int32)
    positions = (group_order[:, slots // block] * block + slots % block).astype(jnp.int32)
    inputs = jnp.transpose(tokens.astype(jnp.float32), (1, 0, 2))
    cot = jnp.transpose(cotangent.astype(jnp.float32), (1, 0, 2))

    def whole(weights, values):
        layer = jax.checkpoint(sequence_layer)

        def step(carry, item):
            return (carry, layer(weights, item[0], item[1]))
        _, result = lax.scan(step, jnp.zeros((), jnp.float32), (values, positions))
        return result
    result, pullback = jax.vjp(whole, params, inputs)
    grads, input_grad = pullback(cot)
    output = jnp.transpose(result, (1, 0, 2)).astype(jnp.bfloat16)
    input_grad = jnp.transpose(input_grad, (1, 0, 2)).astype(jnp.bfloat16)
    return (output, input_grad, grads[0], grads[1], grads[2], grads[3], grads[4], grads[5], grads[6], grads[7], grads[8], grads[9], grads[10])
```

```python
import functools

import jax
import jax.numpy as jnp
from jax import lax
from jax.experimental import pallas as pl
from jax.experimental.pallas import tpu as pltpu
from jax.sharding import PartitionSpec as P

H = 16
HD = 128


EPS = 1e-06
THETA = 500000.0
LOG2E = 1.4426950408889634
NEG = -1e30
SHARE = 64
LONG = 2000
F32 = jnp.float32
BF16 = jnp.bfloat16


def plain(left, right):
    return jnp.dot(left, right, preferred_element_type=F32)


def times_trans(left, right):
    return lax.dot_general(left, right, (((1,), (1,)), ((), ())), preferred_element_type=F32)


def row_dot(left, right):
    return lax.dot_general(left, right, (((0,), (0,)), ((), ())), preferred_element_type=F32)


def swap(value, axis, step):
    count = lax.axis_size(axis)
    return lax.ppermute(value, axis, [(i, i ^ step) for i in range(count)])


def tensor_sum(value):
    if lax.axis_size("tensor") == 2:
        return value.astype(F32) + swap(value, "tensor", 1).astype(F32)
    return lax.psum(value, "tensor").astype(F32)


def vmem(megabytes):
    return pltpu.CompilerParams(vmem_limit_bytes=megabytes * 1024 * 1024)


def after(value, *gates):
    return lax.optimization_barrier((value, gates))[0]


def tensor_list(value):
    if lax.axis_size("tensor") == 2:
        return [value, swap(value, "tensor", 1)]
    return [lax.psum(value, "tensor")]


def tensor_all(value):
    count = lax.axis_size("tensor")
    if count == 2:
        return [value, swap(value, "tensor", 1)]
    every = lax.all_gather(value, "tensor", axis=0)
    return [every[i] for i in range(count)]


def cost(flops, nbytes, exps=0, weight=1):
    flops, nbytes = flops * weight, nbytes * weight
    return pl.CostEstimate(
        flops=int(flops) // SHARE, bytes_accessed=int(nbytes) // SHARE, transcendentals=int(exps) // SHARE
    )


def rms(value):
    return lax.rsqrt(jnp.mean(value * value, axis=-1, keepdims=True) + EPS)


def half_turn(value):
    return pltpu.roll(value, HD // 2, 1)


def turned_back(grad, cosine, sine):
    return grad * cosine - half_turn(grad) * sine


def col_slice(col_ref, s, h):
    return pl.ds(pl.multiple_of(col_ref[s] + h * HD, HD), HD)


def pieces_kernel(wide, col_ref, x_ref, w_ref, *outs):
    x = x_ref[...]
    for s, out in enumerate(outs):
        cols = pl.ds(pl.multiple_of(col_ref[s], HD), wide)
        out[...] = plain(x, w_ref[:, cols]).astype(BF16)


def project_pieces(col, x, weight, share=1):
    rows, depth = x.shape
    width = weight.shape[1]
    n_ctx = col.shape[0]
    wide = width // n_ctx
    tile = min(256, rows)
    return pl.pallas_call(
        functools.partial(pieces_kernel, wide),
        grid_spec=pltpu.PrefetchScalarGridSpec(
            num_scalar_prefetch=1,
            grid=(rows // tile,),
            in_specs=[
                pl.BlockSpec((tile, depth), lambda i, col: (i, 0)),
                pl.BlockSpec((depth, width), lambda i, col: (0, 0)),
            ],
            out_specs=[pl.BlockSpec((tile, wide), lambda i, col: (i, 0))] * n_ctx,
        ),
        out_shape=[jax.ShapeDtypeStruct((rows, wide), BF16)] * n_ctx,
        compiler_params=vmem(32),
        cost_estimate=cost(2 * rows * depth * width, 2 * (rows * depth + depth * width), weight=share),
    )(col, x, weight)


def qk_kernel(x_ref, qw_ref, kw_ref, q_ref, k_ref, sums_ref, q_s, k_s):
    step = pl.program_id(0)
    x = x_ref[...]
    lanes = 128
    for w_ref, out_ref, total in ((qw_ref, q_ref, q_s), (kw_ref, k_ref, k_s)):
        raw = plain(x, w_ref[...])
        out_ref[...] = raw
        square = raw * raw
        part = square[:, :lanes]
        for i in range(1, raw.shape[1] // lanes):
            part += square[:, i * lanes : (i + 1) * lanes]

        @pl.when(step == 0)
        def _():
            total[...] = part

        @pl.when(step > 0)
        def _():
            total[...] += part

    @pl.when(step == pl.num_programs(0) - 1)
    def _():
        sums_ref[0:1, :] = jnp.sum(q_s[...].T, axis=0, keepdims=True)
        sums_ref[1:2, :] = jnp.sum(k_s[...].T, axis=0, keepdims=True)


def qk_project(x, q_weight, k_weight):
    rows, depth = x.shape
    width = q_weight.shape[1]
    tile = min(256, width)
    column = lambda i: (0, i)
    return pl.pallas_call(
        qk_kernel,
        grid=(width // tile,),
        in_specs=[pl.BlockSpec((rows, depth), lambda i: (0, 0))]
        + [pl.BlockSpec((depth, tile), column)] * 2,
        out_specs=[pl.BlockSpec((rows, tile), column)] * 2
        + [pl.BlockSpec((2, rows), lambda i: (0, 0))],
        out_shape=[jax.ShapeDtypeStruct((rows, width), F32)] * 2
        + [jax.ShapeDtypeStruct((2, rows), F32)],
        scratch_shapes=[pltpu.VMEM((rows, 128), F32)] * 2,
        compiler_params=vmem(32),
        cost_estimate=cost(4 * rows * depth * width, 2 * rows * depth + 4 * depth * width + 8 * rows * width),
    )(x, q_weight, k_weight)


def head_prep_kernel(n_ctx, nh, col_ref, q_ref, k_ref, v_ref, qs_ref, ks_ref, qg_ref, kg_ref, cos_ref, sin_ref, *outs):
    cosine = cos_ref[...]
    sine = sin_ref[...]
    q_scale = qs_ref[...]
    k_scale = ks_ref[...]
    for h in range(nh):
        for s in range(n_ctx):
            cols = col_slice(col_ref, s, h)
            out = outs[h * n_ctx + s]
            q = q_ref[:, cols] * q_scale * qg_ref[:, cols]
            out[0] = (q * cosine + half_turn(q) * sine).astype(BF16)
            k = k_ref[:, cols] * k_scale * kg_ref[:, cols]
            out[1] = (k * cosine + half_turn(k) * sine).astype(BF16)
            out[2] = v_ref[:, cols]


def head_prep(col, q_raw, k_raw, value, q_scale, k_scale, q_gain, k_gain, cosine, sine, n_ctx, nh):
    rows, width = q_raw.shape
    tile = min(256, rows)
    row = lambda i, col: (i, 0)
    fixed = lambda i, col: (0, 0)
    return pl.pallas_call(
        functools.partial(head_prep_kernel, n_ctx, nh),
        grid_spec=pltpu.PrefetchScalarGridSpec(
            num_scalar_prefetch=1,
            grid=(rows // tile,),
            in_specs=[pl.BlockSpec((tile, width), row)] * 3
            + [pl.BlockSpec((tile, 1), row)] * 2
            + [pl.BlockSpec((1, width), fixed)] * 2
            + [pl.BlockSpec((tile, HD), row)] * 2,
            out_specs=[pl.BlockSpec((3, tile, HD), lambda i, col: (0, i, 0))] * (n_ctx * nh),
        ),
        out_shape=[jax.ShapeDtypeStruct((3, rows, HD), BF16)] * (n_ctx * nh),
        compiler_params=vmem(32),
        cost_estimate=cost(12 * rows * width, 12 * rows * width),
    )(col, q_raw, k_raw, value, q_scale, k_scale, q_gain, k_gain, cosine, sine)


def back_sums_kernel(n_ctx, head, col_ref, *refs):
    parts = refs[:n_ctx]
    ins = refs[n_ctx : 3 * n_ctx]
    qs_ref, ks_ref, qg_ref, kg_ref, cos_ref, sin_ref = refs[3 * n_ctx : -3]
    sums_ref, qgain_ref, kgain_ref = refs[-3:]
    cosine = cos_ref[...]
    sine = sin_ref[...]
    q_scale = qs_ref[...]
    k_scale = ks_ref[...]

    @pl.when(pl.program_id(0) == 0)
    def _():
        qgain_ref[...] = jnp.zeros_like(qgain_ref)
        kgain_ref[...] = jnp.zeros_like(kgain_ref)

    q_total = jnp.zeros_like(cosine)
    k_total = jnp.zeros_like(cosine)
    for s in range(n_ctx):
        cols = col_slice(col_ref, s, head)
        q_term = turned_back(parts[s][0].astype(F32), cosine, sine) * ins[2 * s][...]
        q_total += q_term * qg_ref[:, cols]
        qgain_ref[:, cols] += jnp.sum(q_term * q_scale, axis=0, keepdims=True)
        k_term = turned_back(parts[s][1].astype(F32), cosine, sine) * ins[2 * s + 1][...]
        k_total += k_term * kg_ref[:, cols]
        kgain_ref[:, cols] += jnp.sum(k_term * k_scale, axis=0, keepdims=True)
    sums_ref[0:1, :] = jnp.sum(q_total.T, axis=0, keepdims=True)
    sums_ref[1:2, :] = jnp.sum(k_total.T, axis=0, keepdims=True)


def back_sums(col, parts, q_raw, k_raw, q_scale, k_scale, q_gain, k_gain, cosine, sine, head):
    n_ctx = len(parts)
    rows, width = q_raw.shape
    tile = min(256, rows)
    row = lambda i, col: (i, 0)
    fixed = lambda i, col: (0, 0)
    in_specs = [pl.BlockSpec((2, tile, HD), lambda i, col: (0, i, 0)) for _ in parts]
    operands = list(parts)
    for s in range(n_ctx):
        for raw in (q_raw, k_raw):
            in_specs.append(pl.BlockSpec((tile, HD), lambda i, col, s=s: (i, col[s] // HD + head)))
            operands.append(raw)
    return pl.pallas_call(
        functools.partial(back_sums_kernel, n_ctx, head),
        grid_spec=pltpu.PrefetchScalarGridSpec(
            num_scalar_prefetch=1,
            grid=(rows // tile,),
            in_specs=in_specs
            + [pl.BlockSpec((tile, 1), row)] * 2
            + [pl.BlockSpec((1, width), fixed)] * 2
            + [pl.BlockSpec((tile, HD), row)] * 2,
            out_specs=[pl.BlockSpec((2, tile), lambda i, col: (0, i))]
            + [pl.BlockSpec((1, width), fixed)] * 2,
        ),
        out_shape=[jax.ShapeDtypeStruct((2, rows), F32)]
        + [jax.ShapeDtypeStruct((1, width), F32)] * 2,
        compiler_params=vmem(32),
        cost_estimate=cost(20 * rows * n_ctx * HD, 12 * rows * n_ctx * HD, weight=20000),
    )(col, *operands, q_scale, k_scale, q_gain, k_gain, cosine, sine)


def back_prep_kernel(n_ctx, nh, col_ref, *refs):
    parts = refs[: n_ctx * nh]
    (q_ref, k_ref, qs_ref, ks_ref, qm_ref, km_ref, qg_ref, kg_ref, cos_ref, sin_ref) = refs[
        n_ctx * nh : n_ctx * nh + 10
    ]
    qw_ref, kw_ref, vw_ref = refs[-5:-2]
    d_ref, in_ref = refs[-2:]
    cosine = cos_ref[...]
    sine = sin_ref[...]
    q_scale = qs_ref[...]
    k_scale = ks_ref[...]
    q_mean = qm_ref[...]
    k_mean = km_ref[...]
    for h in range(nh):
        for s in range(n_ctx):
            cols = col_slice(col_ref, s, h)
            part = parts[h * n_ctx + s]
            dq = turned_back(part[0].astype(F32), cosine, sine) * qg_ref[:, cols]
            d_ref[0, :, cols] = (dq * q_scale - q_ref[:, cols] * q_mean).astype(BF16)
            dk = turned_back(part[1].astype(F32), cosine, sine) * kg_ref[:, cols]
            d_ref[1, :, cols] = (dk * k_scale - k_ref[:, cols] * k_mean).astype(BF16)
            d_ref[2, :, cols] = part[2]
    total = times_trans(d_ref[0], qw_ref[...])
    total += times_trans(d_ref[1], kw_ref[...])
    total += times_trans(d_ref[2], vw_ref[...])
    in_ref[...] = total.astype(BF16)


def back_prep(
    c, count, col, parts, q_raw, k_raw, q_scale, k_scale, q_mean, k_mean, q_gain, k_gain, cosine, sine,
    q_weight, k_weight, v_weight, n_ctx, nh
):
    width = q_raw.shape[1]
    depth = q_weight.shape[0]
    tile = min(256, count)
    first = c * count // tile
    row = lambda i, col: (first + i, 0)
    here = lambda i, col: (i, 0)
    fixed = lambda i, col: (0, 0)
    return pl.pallas_call(
        functools.partial(back_prep_kernel, n_ctx, nh),
        grid_spec=pltpu.PrefetchScalarGridSpec(
            num_scalar_prefetch=1,
            grid=(count // tile,),
            in_specs=[pl.BlockSpec((3, tile, HD), lambda i, col: (0, first + i, 0))] * (n_ctx * nh)
            + [pl.BlockSpec((tile, width), row)] * 2
            + [pl.BlockSpec((tile, 1), row)] * 4
            + [pl.BlockSpec((1, width), fixed)] * 2
            + [pl.BlockSpec((tile, HD), row)] * 2
            + [pl.BlockSpec((depth, width), fixed)] * 3,
            out_specs=[
                pl.BlockSpec((3, tile, width), lambda i, col: (0, i, 0)),
                pl.BlockSpec((tile, depth), here),
            ],
        ),
        out_shape=[
            jax.ShapeDtypeStruct((3, count, width), BF16),
            jax.ShapeDtypeStruct((count, depth), BF16),
        ],
        compiler_params=vmem(56),
        cost_estimate=cost(6 * count * width * depth, 6 * width * depth + 20 * count * width),
    )(
        col, *parts, q_raw, k_raw, q_scale, k_scale, q_mean, k_mean, q_gain, k_gain, cosine, sine,
        q_weight, k_weight, v_weight,
    )


def causal(keys, queries, first):
    key = lax.broadcasted_iota(jnp.int32, (keys, queries), 0) + first
    query = lax.broadcasted_iota(jnp.int32, (keys, queries), 1)
    return key <= query


def by_eights(value):
    return value.reshape(value.shape[0] // 8, 8, value.shape[1])


def attend_kernel(n_ctx, per, block, sub, wide, place_ref, *refs):
    qkvs = refs[:n_ctx]
    outs = refs[n_ctx : 2 * n_ctx]
    ot_ref, lse_ref, qt_s, k_s, vt_s, score_s = refs[2 * n_ctx :]
    blocks = n_ctx * per
    factor = HD ** (-0.5) * LOG2E

    def spots(g):
        there = pl.ds(pl.multiple_of(place_ref[g] * block, block), block)
        return g // per, slice((g % per) * block, (g % per + 1) * block), there

    for g in range(blocks):
        r, here, there = spots(g)
        qt_s[:, there] = qkvs[r][0, here, :].T
        k_s[there, :] = qkvs[r][1, here, :]
        vt_s[:, there] = qkvs[r][2, here, :].T

    def query_step(i, _):
        mine = pl.ds(pl.multiple_of(i * block, block), block)
        qt = qt_s[:, mine]
        last = i * block // wide

        def part(j, u):
            return pl.ds(pl.multiple_of(j * wide + u * sub, sub), sub)

        def score_step(j, top, masked=False):
            for u in range(wide // sub):
                scores = plain(k_s[part(j, u), :], qt)
                if masked:
                    scores = jnp.where(
                        causal(sub, block, j * wide + u * sub - i * block), scores, NEG
                    )
                score_s[part(j, u), :] = scores
                top = jnp.maximum(top, jnp.max(by_eights(scores), axis=0))
            return top

        top = score_step(last, jnp.full((8, block), NEG, F32), masked=True)
        top = lax.fori_loop(0, last, score_step, top)
        top = jnp.max(top, axis=0, keepdims=True) * factor

        def value_step(j, carry):
            total, acc = carry
            for u in range(wide // sub):
                expo = jnp.exp2(score_s[part(j, u), :] * factor - top)
                total = total + jnp.sum(by_eights(expo), axis=0)
                acc = acc + plain(vt_s[:, part(j, u)], expo.astype(BF16))
            return total, acc

        start = (jnp.zeros((8, block), F32), jnp.zeros((HD, block), F32))
        total, acc = lax.fori_loop(0, last + 1, value_step, start)
        total = jnp.sum(total, axis=0, keepdims=True)
        ot_ref[:, mine] = acc / total
        lse_ref[:, mine] = top + jnp.log2(total)
        return 0

    lax.fori_loop(0, blocks, query_step, 0)
    for g in range(blocks):
        r, here, there = spots(g)
        outs[r][here, :] = ot_ref[:, there].T.astype(BF16)


def attend(place, qkvs, block):
    n_ctx = len(qkvs)
    rows = qkvs[0].shape[1]
    per = rows // block
    length = n_ctx * rows
    whole = lambda: pl.BlockSpec(memory_space=pltpu.VMEM)
    return pl.pallas_call(
        functools.partial(attend_kernel, n_ctx, per, block, min(256, block), rows),
        in_specs=[pl.BlockSpec(memory_space=pltpu.SMEM)] + [whole() for _ in qkvs],
        out_specs=[whole() for _ in range(n_ctx + 2)],
        out_shape=[jax.ShapeDtypeStruct((rows, HD), BF16)] * n_ctx
        + [jax.ShapeDtypeStruct((HD, length), F32), jax.ShapeDtypeStruct((1, length), F32)],
        scratch_shapes=[
            pltpu.VMEM((HD, length), BF16),
            pltpu.VMEM((length, HD), BF16),
            pltpu.VMEM((HD, length), BF16),
            pltpu.VMEM((length, block), F32),
        ],
        compiler_params=vmem(40),
        cost_estimate=cost(6 * length * length * HD, 12 * length * HD, length * length // 2),
    )(place, *qkvs)


def attend_back_kernel(n_ctx, per, block, sub, wide, place_ref, *refs):
    blocks = n_ctx * per
    qkvs = refs[:n_ctx]
    d_outs = refs[n_ctx : n_ctx + blocks]
    rest = refs[n_ctx + blocks :]
    ot_ref, lse_ref = rest[:2]
    grads = rest[2 : 2 + n_ctx]
    q_s, qt_s, k_s, kt_s, v_s, do_s, dot_s, delta_s, dqt_s, dk_s, dv_s = rest[2 + n_ctx :]
    scale = HD ** (-0.5)
    factor = scale * LOG2E

    def spots(g):
        there = pl.ds(pl.multiple_of(place_ref[g] * block, block), block)
        return g // per, slice((g % per) * block, (g % per + 1) * block), there

    for g in range(blocks):
        r, here, there = spots(g)
        queries = qkvs[r][0, here, :]
        q_s[there, :] = queries
        qt_s[:, there] = queries.T
        keys = qkvs[r][1, here, :]
        k_s[there, :] = keys
        kt_s[:, there] = keys.T
        v_s[there, :] = qkvs[r][2, here, :]
        d_out = d_outs[g][...]
        do_s[there, :] = d_out
        turned = d_out.T
        dot_s[:, there] = turned
        delta_s[:, there] = jnp.sum(turned.astype(F32) * ot_ref[:, there], axis=0, keepdims=True)
    dqt_s[...] = jnp.zeros_like(dqt_s)
    subs = block // sub
    tiles = blocks * block // wide

    def key_step(j, _):
        part = lambda u: pl.ds(pl.multiple_of(j * block + u * sub, sub), sub)
        first = j * block // wide

        def query_step(i, carry, masked=False):
            theirs = pl.ds(pl.multiple_of(i * wide, wide), wide)
            lse = lse_ref[:, theirs]
            delta = delta_s[:, theirs]
            dqt = dqt_s[:, theirs]
            sums = []
            for u in range(subs):
                dk, dv = carry[u]
                scores = plain(k_s[part(u), :], qt_s[:, theirs])
                d_probs = plain(v_s[part(u), :], dot_s[:, theirs])
                probs = jnp.exp2(scores * factor - lse)
                if masked:
                    probs = jnp.where(causal(sub, wide, j * block + u * sub - i * wide), probs, 0.0)
                d_scores = (probs * (d_probs - delta)).astype(BF16)
                dv = dv + plain(probs.astype(BF16), do_s[theirs, :])
                dk = dk + plain(d_scores, q_s[theirs, :])
                dqt = dqt + plain(kt_s[:, part(u)], d_scores)
                sums.append((dk, dv))
            dqt_s[:, theirs] = dqt
            return tuple(sums)

        zero = jnp.zeros((sub, HD), F32)
        carry = query_step(first, ((zero, zero),) * subs, masked=True)
        carry = lax.fori_loop(first + 1, tiles, query_step, carry)
        for u in range(subs):
            dk_s[part(u), :] = carry[u][0]
            dv_s[part(u), :] = carry[u][1]
        return 0

    lax.fori_loop(0, blocks, key_step, 0)
    for g in range(blocks):
        r, here, there = spots(g)
        out = grads[r]
        out[0, here, :] = (dqt_s[:, there].T * scale).astype(BF16)
        out[1, here, :] = (dk_s[there, :] * scale).astype(BF16)
        out[2, here, :] = dv_s[there, :].astype(BF16)


def attend_back(place, qkvs, d_outs, head, out_t, lse, block):
    n_ctx = len(qkvs)
    rows = qkvs[0].shape[1]
    per = rows // block
    length = n_ctx * rows
    whole = lambda: pl.BlockSpec(memory_space=pltpu.VMEM)
    return pl.pallas_call(
        functools.partial(attend_back_kernel, n_ctx, per, block, min(256, block), block),
        grid=(1,),
        in_specs=[pl.BlockSpec(memory_space=pltpu.SMEM)]
        + [whole() for _ in qkvs]
        + [pl.BlockSpec((block, HD), lambda i: (0, head)) for _ in d_outs]
        + [whole(), whole()],
        out_specs=[whole() for _ in range(n_ctx)],
        out_shape=[jax.ShapeDtypeStruct((3, rows, HD), BF16)] * n_ctx,
        scratch_shapes=[
            pltpu.VMEM((length, HD), BF16),
            pltpu.VMEM((HD, length), BF16),
            pltpu.VMEM((length, HD), BF16),
            pltpu.VMEM((HD, length), BF16),
            pltpu.VMEM((length, HD), BF16),
            pltpu.VMEM((length, HD), BF16),
            pltpu.VMEM((HD, length), BF16),
            pltpu.VMEM((1, length), F32),
            pltpu.VMEM((HD, length), F32),
            pltpu.VMEM((length, HD), F32),
            pltpu.VMEM((length, HD), F32),
        ],
        compiler_params=vmem(48),
        cost_estimate=cost(8 * length * length * HD, 20 * length * HD, length * length // 2),
    )(place, *qkvs, *d_outs, out_t, lse)


def join_kernel(nh, per, block, col_ref, *refs):
    n_parts = len(refs) - per
    parts, outs = refs[:n_parts], refs[n_parts:]
    for j, part in enumerate(parts):
        cols = col_slice(col_ref, j // nh, j % nh)
        for c in range(per):
            outs[c][:, cols] = part[c * block : (c + 1) * block, :]


def join_heads(col, parts, nh, per):
    rows = parts[0].shape[0]
    block = rows // per
    width = len(parts) * HD
    whole = lambda: pl.BlockSpec(memory_space=pltpu.VMEM)
    return pl.pallas_call(
        functools.partial(join_kernel, nh, per, block),
        in_specs=[pl.BlockSpec(memory_space=pltpu.SMEM)] + [whole() for _ in parts],
        out_specs=[whole() for _ in range(per)],
        out_shape=[jax.ShapeDtypeStruct((block, width), BF16)] * per,
        compiler_params=vmem(24),
        cost_estimate=cost(0, 4 * rows * width),
    )(col, *parts)


def branch_kernel(count, me_ref, *refs):
    atts, weights = refs[:count], refs[count : 2 * count]
    x_ref, gain_ref, branch_ref, low_ref = refs[2 * count :]

    def add_up(order):
        branch = times_trans(atts[order[0]][...], weights[order[0]][...])
        for i in order[1:]:
            branch = branch + times_trans(atts[i][...], weights[i][...])
        branch_ref[...] = branch
        hidden = x_ref[...].astype(F32) + branch * rms(branch) * gain_ref[...]
        low_ref[...] = hidden.astype(BF16)

    if count == 2:
        pl.when(me_ref[0] == 0)(lambda: add_up((0, 1)))
        pl.when(me_ref[0] != 0)(lambda: add_up((1, 0)))
    else:
        add_up(range(count))


def branch_rows(c, atts, weights, tokens, gain):
    rows, wide = atts[0].shape
    depth = weights[0].shape[0]
    tile = min(256, rows)
    first = c * rows // tile
    fixed = lambda i: (0, 0)
    here = lambda i: (i, 0)
    return pl.pallas_call(
        functools.partial(branch_kernel, len(atts)),
        grid=(rows // tile,),
        in_specs=[pl.BlockSpec(memory_space=pltpu.SMEM)]
        + [pl.BlockSpec((tile, wide), here) for _ in atts]
        + [pl.BlockSpec((depth, wide), fixed) for _ in weights]
        + [pl.BlockSpec((tile, depth), lambda i: (first + i, 0)), pl.BlockSpec((1, depth), fixed)],
        out_specs=[pl.BlockSpec((tile, depth), here)] * 2,
        out_shape=[
            jax.ShapeDtypeStruct((rows, depth), F32),
            jax.ShapeDtypeStruct((rows, depth), BF16),
        ],
        compiler_params=vmem(48),
        cost_estimate=cost(2 * rows * wide * depth * len(atts), 8 * rows * depth + 2 * depth * wide * len(atts)),
    )(lax.axis_index("tensor").reshape(1).astype(jnp.int32), *atts, *weights, tokens, gain)


def middle_kernel(count, *refs):
    parts = refs[:count]
    cot_ref, branch_ref, x_ref, again_ref, mgain_ref = refs[count : count + 5]
    out_ref, dmixed_ref, gain_ref = refs[-3:]
    mixed = parts[0][...].astype(F32)
    for part in parts[1:]:
        mixed = mixed + part[...].astype(F32)
    branch = branch_ref[...]
    hidden = x_ref[...].astype(F32) + branch * rms(branch) * again_ref[...]
    scale = rms(mixed)
    mgain = mgain_ref[...]
    normed = mixed * scale
    out_ref[...] = (hidden + normed * mgain).astype(BF16)
    grad = cot_ref[...].astype(F32)

    @pl.when(pl.program_id(0) == 0)
    def _():
        gain_ref[...] = jnp.zeros_like(gain_ref)

    gain_ref[...] += jnp.sum(grad * normed, axis=0, keepdims=True)
    weighted = grad * mgain
    mean = jnp.mean(weighted * normed, axis=-1, keepdims=True)
    dmixed_ref[...] = (scale * (weighted - normed * mean)).astype(BF16)


def middle_rows(c, parts, cot, branch, tokens, attn_gain, mlp_gain, output):
    rows, width = parts[0].shape
    tile = min(128, rows)
    first = c * rows // tile
    here = lambda i: (i, 0)
    there = lambda i: (first + i, 0)
    fixed = lambda i: (0, 0)
    return pl.pallas_call(
        functools.partial(middle_kernel, len(parts)),
        grid=(rows // tile,),
        in_specs=[pl.BlockSpec((tile, width), here) for _ in parts]
        + [
            pl.BlockSpec((tile, width), there),
            pl.BlockSpec((tile, width), here),
            pl.BlockSpec((tile, width), there),
            pl.BlockSpec((1, width), fixed),
            pl.BlockSpec((1, width), fixed),
        ]
        + [pl.BlockSpec(memory_space=pl.ANY) for _ in output],
        out_specs=[
            pl.BlockSpec((tile, width), there),
            pl.BlockSpec((tile, width), here),
            pl.BlockSpec((1, width), fixed),
        ],
        out_shape=[
            jax.ShapeDtypeStruct(tokens.shape, BF16),
            jax.ShapeDtypeStruct((rows, width), BF16),
            jax.ShapeDtypeStruct((1, width), F32),
        ],
        input_output_aliases={len(parts) + 5: 0} if output else {},
        compiler_params=vmem(32),
        cost_estimate=cost(30 * rows * width, 16 * rows * width),
    )(*parts, cot, branch, tokens, attn_gain, mlp_gain, *output)


def total_kernel(count, *refs):
    total = refs[0][...].astype(F32)
    for part in refs[1:count]:
        total = total + part[...].astype(F32)
    refs[-1][...] = total.astype(BF16)


def total_rows(c, cot, parts, output):
    rows, width = parts[0].shape
    tile = min(128, rows)
    first = c * rows // tile
    there = lambda i: (first + i, 0)
    return pl.pallas_call(
        functools.partial(total_kernel, 1 + len(parts)),
        grid=(rows // tile,),
        in_specs=[pl.BlockSpec((tile, width), there)]
        + [pl.BlockSpec((tile, width), lambda i: (i, 0)) for _ in parts]
        + [pl.BlockSpec(memory_space=pl.ANY) for _ in output],
        out_specs=pl.BlockSpec((tile, width), there),
        out_shape=jax.ShapeDtypeStruct(cot.shape, BF16),
        input_output_aliases={1 + len(parts): 0} if output else {},
        compiler_params=vmem(32),
        cost_estimate=cost(6 * rows * width, 12 * rows * width),
    )(cot, *parts, *output)


def last_kernel(count, *refs):
    parts = refs[:count]
    cot_ref, branch_ref, again_ref, dbranch_ref, gain_ref = refs[count:]
    total = parts[0][...].astype(F32)
    for part in parts[1:]:
        total = total + part[...].astype(F32)
    d_hidden = cot_ref[...].astype(F32) + total
    branch = branch_ref[...]
    scale = rms(branch)
    normed = branch * scale

    @pl.when(pl.program_id(0) == 0)
    def _():
        gain_ref[...] = jnp.zeros_like(gain_ref)

    gain_ref[...] += jnp.sum(d_hidden * normed, axis=0, keepdims=True)
    weighted = d_hidden * again_ref[...]
    mean = jnp.mean(weighted * normed, axis=-1, keepdims=True)
    dbranch_ref[...] = (scale * (weighted - normed * mean)).astype(BF16)


def last_rows(c, parts, cot, branch, attn_gain):
    rows, width = parts[0].shape
    tile = min(128, rows)
    first = c * rows // tile
    here = lambda i: (i, 0)
    there = lambda i: (first + i, 0)
    fixed = lambda i: (0, 0)
    return pl.pallas_call(
        functools.partial(last_kernel, len(parts)),
        grid=(rows // tile,),
        in_specs=[pl.BlockSpec((tile, width), here) for _ in parts]
        + [
            pl.BlockSpec((tile, width), there),
            pl.BlockSpec((tile, width), here),
            pl.BlockSpec((1, width), fixed),
        ],
        out_specs=[pl.BlockSpec((tile, width), here), pl.BlockSpec((1, width), fixed)],
        out_shape=[
            jax.ShapeDtypeStruct((rows, width), BF16),
            jax.ShapeDtypeStruct((1, width), F32),
        ],
        compiler_params=vmem(32),
        cost_estimate=cost(20 * rows * width, 12 * rows * width, weight=LONG if c == 0 else 1),
    )(*parts, cot, branch, attn_gain)


def forward_kernel(sub, x_ref, gw_ref, uw_ref, dw_ref, slope_ref, silu_ref, inner_ref, mixed_ref, acc):
    step = pl.program_id(0)
    x = x_ref[...]
    for t in range(gw_ref.shape[1] // sub):
        span = slice(t * sub, (t + 1) * sub)
        gate = plain(x, gw_ref[:, span])
        up = plain(x, uw_ref[:, span])
        sigmoid = 1.0 / (1.0 + jnp.exp2(gate * (-LOG2E)))
        silu = gate * sigmoid
        inner_ref[:, span] = (silu * up).astype(BF16)
        silu_ref[:, span] = silu.astype(BF16)
        slope_ref[:, span] = (up * (sigmoid + silu * (1.0 - sigmoid))).astype(BF16)
    product = times_trans(inner_ref[...], dw_ref[...])

    @pl.when(step == 0)
    def _():
        acc[...] = product

    @pl.when(step > 0)
    def _():
        acc[...] += product

    @pl.when(step == pl.num_programs(0) - 1)
    def _():
        mixed_ref[...] = acc[...].astype(BF16)


def forward_rows(x, gate_weight, up_weight, down_weight):
    rows, depth = x.shape
    units = gate_weight.shape[1]
    tile = min(512, units)
    column = lambda i: (0, i)
    fixed = lambda i: (0, 0)
    return pl.pallas_call(
        functools.partial(forward_kernel, min(256, tile)),
        grid=(units // tile,),
        in_specs=[pl.BlockSpec((rows, depth), fixed)] + [pl.BlockSpec((depth, tile), column)] * 3,
        out_specs=[pl.BlockSpec((rows, tile), column)] * 3 + [pl.BlockSpec((rows, depth), fixed)],
        out_shape=[jax.ShapeDtypeStruct((rows, units), BF16)] * 3
        + [jax.ShapeDtypeStruct((rows, depth), BF16)],
        scratch_shapes=[pltpu.VMEM((rows, depth), F32)],
        compiler_params=vmem(48),
        cost_estimate=cost(6 * rows * depth * units, 6 * depth * units + 6 * rows * units, rows * units),
    )(x, gate_weight, up_weight, down_weight)


def backward_kernel(sub, d_ref, dw_ref, gw_ref, uw_ref, slope_ref, silu_ref, both_ref, dhid_ref, acc):
    step = pl.program_id(0)
    d_mixed = d_ref[...]
    for t in range(dw_ref.shape[1] // sub):
        span = slice(t * sub, (t + 1) * sub)
        d_inner = plain(d_mixed, dw_ref[:, span])
        both_ref[0, :, span] = (d_inner * slope_ref[:, span].astype(F32)).astype(BF16)
        both_ref[1, :, span] = (d_inner * silu_ref[:, span].astype(F32)).astype(BF16)
    product = times_trans(both_ref[0], gw_ref[...]) + times_trans(both_ref[1], uw_ref[...])

    @pl.when(step == 0)
    def _():
        acc[...] = product

    @pl.when(step > 0)
    def _():
        acc[...] += product

    @pl.when(step == pl.num_programs(0) - 1)
    def _():
        dhid_ref[...] = acc[...].astype(BF16)


def backward_rows(d_mixed, down_weight, gate_weight, up_weight, slope, silu):
    rows, depth = d_mixed.shape
    units = gate_weight.shape[1]
    tile = min(512, units)
    column = lambda i: (0, i)
    fixed = lambda i: (0, 0)
    return pl.pallas_call(
        functools.partial(backward_kernel, min(256, tile)),
        grid=(units // tile,),
        in_specs=[pl.BlockSpec((rows, depth), fixed)]
        + [pl.BlockSpec((depth, tile), column)] * 3
        + [pl.BlockSpec((rows, tile), column)] * 2,
        out_specs=[pl.BlockSpec((2, rows, tile), lambda i: (0, 0, i)), pl.BlockSpec((rows, depth), fixed)],
        out_shape=[
            jax.ShapeDtypeStruct((2, rows, units), BF16),
            jax.ShapeDtypeStruct((rows, depth), BF16),
        ],
        scratch_shapes=[pltpu.VMEM((rows, depth), F32)],
        compiler_params=vmem(48),
        cost_estimate=cost(6 * rows * depth * units, 6 * depth * units + 8 * rows * units),
    )(d_mixed, down_weight, gate_weight, up_weight, slope, silu)


def row_steps(first):
    ctx_bits = [("ctx", 1 << i) for i in range(lax.axis_size("ctx").bit_length() - 1)]
    dp_bits = [("dp", 1 << i) for i in range(lax.axis_size("dp").bit_length() - 1)]
    if first == "ctx":
        return ctx_bits + dp_bits
    return ctx_bits[:1] + dp_bits + ctx_bits[1:]


def row_order(steps):
    dp = lax.axis_index("dp")
    ctx = lax.axis_index("ctx")
    order = []
    for j in range(1 << len(steps)):
        flips = {"dp": 0, "ctx": 0}
        for place, (axis, bit) in enumerate(steps):
            if j >> (len(steps) - 1 - place) & 1:
                flips[axis] |= bit
        order.append((dp ^ flips["dp"]) * lax.axis_size("ctx") + (ctx ^ flips["ctx"]))
    return jnp.stack(order).astype(jnp.int32)


def grad_kernel(pieces, chunks, piece, tokens, idx_ref, *refs):
    lefts = refs[: pieces * chunks]
    rights = refs[pieces * chunks : pieces * chunks + chunks]
    outs, turned = refs[pieces * chunks + chunks : -1], refs[-1]

    @pl.when(pl.program_id(0) == 0)
    def _():
        for p in range(pieces):
            for c in range(chunks):
                turned[p * piece : (p + 1) * piece, c * tokens : (c + 1) * tokens] = lefts[
                    p * chunks + c
                ][...].T

    rows = pieces * piece
    share = rows // len(outs)
    step = min(256, rows)
    for m in range(0, rows, step):
        total = None
        for c in range(chunks):
            right = rights[c][0] if len(rights[c].shape) == 3 else rights[c][...]
            term = plain(turned[m : m + step, c * tokens : (c + 1) * tokens], right)
            total = term if total is None else total + term
        total = total.astype(BF16)
        size = min(share, step)
        for i in range(m, m + step, size):
            outs[i // share][i % share : i % share + size, :] = total[i - m : i - m + size]


def grad_rows(index, lefts, rights, split):
    pieces = index.shape[0]
    chunks = len(lefts)
    tokens = rights[0][0].shape[-2]
    piece = lefts[0][0].shape[1] // (lax.axis_size("dp") * lax.axis_size("ctx"))
    width = rights[0][0].shape[-1]
    tile = min(512, width)
    count = width // tile
    rows = pieces * piece
    in_specs = []
    operands = []
    for p in range(pieces):
        for left, c in lefts:
            in_specs.append(pl.BlockSpec((tokens, piece), lambda n, idx, p=p, c=c: (c, idx[p])))
            operands.append(left)
    for right, which in rights:
        if which is None:
            in_specs.append(pl.BlockSpec((tokens, tile), lambda n, idx: (0, n)))
        else:
            in_specs.append(pl.BlockSpec((1, tokens, tile), lambda n, idx, which=which: (which, 0, n)))
        operands.append(right)
    return pl.pallas_call(
        functools.partial(grad_kernel, pieces, chunks, piece, tokens),
        grid_spec=pltpu.PrefetchScalarGridSpec(
            num_scalar_prefetch=1,
            grid=(count,),
            in_specs=in_specs,
            out_specs=[pl.BlockSpec((rows // split, tile), lambda n, idx: (0, n))] * split,
            scratch_shapes=[pltpu.VMEM((rows, chunks * tokens), BF16)],
        ),
        out_shape=[jax.ShapeDtypeStruct((rows // split, width), BF16)] * split,
        compiler_params=vmem(40),
        cost_estimate=cost(
            2 * rows * tokens * chunks * width, 2 * (rows + tokens * chunks) * width + 2 * rows * width
        ),
    )(index, *operands)


def near(value):
    return swap(value, "ctx", 1)


class Gradient:
    def __init__(self, lefts, rights, steps, which=None):
        self.steps = steps
        self.lefts = [left if isinstance(left, tuple) else (left, 0) for left in lefts]
        self.rights = [(right, which) for right in rights]
        index = row_order(steps)
        self.index = index[: index.shape[0] // 2]
        self.place = 1

    def multiply(self, *gates):
        index = after(self.index, *gates)
        self.low, self.high = grad_rows(index, self.lefts, self.rights, 2)
        return self.low

    def step(self, *gates):
        came = swap(self.high, *self.steps[self.place])
        if gates:
            came = after(came, *gates)
        self.place += 1
        if self.place == len(self.steps):
            self.low = self.low.astype(F32) + came.astype(F32)
        else:
            half = self.low.shape[0] // 2
            self.high = (self.low[half:].astype(F32) + came[half:].astype(F32)).astype(BF16)
            self.low = (self.low[:half].astype(F32) + came[:half].astype(F32)).astype(BF16)
        return self.low

    def result(self):
        while self.place < len(self.steps):
            self.step()
        return self.low


class PiecedGradient(Gradient):
    def multiply(self, *gates):
        index = after(self.index, *gates)
        self.blocks = grad_rows(index, self.lefts, self.rights, index.shape[0])
        self.came = {}
        return self.blocks[0]

    def send(self, i, *gates):
        block = self.blocks[len(self.blocks) // 2 + i]
        if gates:
            block = after(block, *gates)
        self.came[i] = swap(block, *self.steps[self.place])
        return self.came[i]

    def add(self, *gates):
        half = len(self.blocks) // 2
        for i in range(half):
            if i not in self.came:
                self.send(i)
        kind = F32 if half == 1 else BF16
        self.blocks = [
            (self.blocks[i].astype(F32) + after(self.came[i], *gates).astype(F32)).astype(kind)
            for i in range(half)
        ]
        self.came = {}
        self.place += 1
        return self.blocks[0]

    def result(self):
        while len(self.blocks) > 1:
            self.add()
        return self.blocks[0]


def on_device(
    tokens,
    q_weight,
    k_weight,
    v_weight,
    o_weight,
    gate_weight,
    up_weight,
    down_weight,
    q_gain,
    k_gain,
    attn_gain,
    mlp_gain,
    group_order,
    cotangent,
):
    local, seqs, width = tokens.shape
    rows = local * seqs
    n_ctx = lax.axis_size("ctx")
    me = lax.axis_index("ctx")
    heads_here = q_weight.shape[1] // HD
    nh = heads_here // n_ctx
    features = H * HD
    groups = group_order.shape[1]
    length = local * n_ctx
    block = length // groups
    per = local // block
    flat = tokens.reshape(rows, width)
    cot = cotangent.reshape(rows, width)
    again = attn_gain.reshape(1, -1)
    mgain = mlp_gain.reshape(1, -1)

    others = [me ^ s for s in range(n_ctx)]
    rel = jnp.stack(others).astype(jnp.int32)
    col = rel * (nh * HD)
    order = group_order.reshape(groups)
    place = jnp.concatenate(
        [lax.dynamic_slice_in_dim(order, o * per, per, 0) for o in others]
    ).astype(jnp.int32)

    y_first = row_steps("ctx")
    z_first = row_steps("dp")

    query_raw, key_raw, sums = qk_project(flat, q_weight, k_weight)
    value = plain(after(flat, sums), v_weight).astype(BF16)
    scales = lax.rsqrt(tensor_sum(sums) / features + EPS)
    q_scale = scales[0][:, None]
    k_scale = scales[1][:, None]
    own_order = lax.dynamic_slice_in_dim(order, me * per, per, 0)
    query_pos = (own_order[:, None] * block + jnp.arange(block, dtype=jnp.int32)[None, :]).reshape(local)
    freq = jnp.power(THETA, -jnp.arange(HD // 2, dtype=F32) * 2.0 / HD)
    angle = query_pos.astype(F32)[:, None] * freq
    cosine = jnp.cos(angle)
    sine = jnp.sin(angle)
    cosine = jnp.concatenate([cosine, cosine], axis=1)
    sine = jnp.concatenate([-sine, sine], axis=1)
    qg = q_gain.reshape(1, -1)
    kg = k_gain.reshape(1, -1)
    packed = head_prep(col, query_raw, key_raw, value, q_scale, k_scale, qg, kg, cosine, sine, n_ctx, nh)
    qkvs = []
    for h in range(nh):
        mine = packed[h * n_ctx : (h + 1) * n_ctx]
        qkvs.append([mine[0]] + [swap(mine[s], "ctx", s) for s in range(1, n_ctx)])

    o_weights = tensor_all(after(o_weight, packed[0]))

    attended = []
    returned = []
    for h in range(nh):
        result = attend(place, qkvs[h], block)
        attended.append(result[n_ctx:])
        returned.append([result[0]] + [swap(result[s], "ctx", s) for s in range(1, n_ctx)])
    att = join_heads(col, [returned[h][s] for s in range(n_ctx) for h in range(nh)], nh, per)

    chunks = range(per)
    with_near = lambda values: list(values) + [near(v) for v in values]
    branch, lowered, slope, silu, inner, mixed = [], [], [], [], [], []
    gate = None
    for c in chunks:
        b, low = branch_rows(c, tensor_all(att[c]), o_weights, flat, again)
        branch.append(b)
        lowered.append(low)
        if gate is not None:
            low = after(low, gate)
        a, s, i, m = forward_rows(low, gate_weight, up_weight, down_weight)
        gate = m
        slope.append(a)
        silu.append(s)
        inner.append(i)
        mixed.append(tensor_list(m))
    output, d_mixed, mlp_terms, d_both, hid = [], [], [], [], []
    d_branch, attn_terms, d_outs = [], [], []

    def last(c, *gates):
        hid[c][0] = after(hid[c][0], *gates)
        d, term = last_rows(c, hid[c], cot, branch[c], again)
        d_branch.append(d)
        attn_terms.append(term)
        pieces = project_pieces(col, d, o_weight, LONG if c == 0 else 1)
        d_outs.append([pieces[0]] + [swap(pieces[s], "ctx", s) for s in range(1, n_ctx)])
        return pieces[0]

    for c in chunks:
        if c:
            mixed[c][0] = after(mixed[c][0], gate)
        out, d, term = middle_rows(c, mixed[c], cot, branch[c], flat, again, mgain, output)
        output = [out]
        d_mixed.append(d)
        mlp_terms.append(term)
        if c == per - 1:
            down_grad = PiecedGradient(with_near(d_mixed), with_near(inner), y_first)
            d = after(d, down_grad.multiply())
        g, h = backward_rows(d, down_weight, gate_weight, up_weight, slope[c], silu[c])
        gate = h
        d_both.append(g)
        hid.append(tensor_list(h))
    for c in range(per - 1):
        gate = last(c, gate)
    low_all, both_all = with_near(lowered), with_near(d_both)
    gate_grad = PiecedGradient(low_all, both_all, z_first, 0)
    gate = gate_grad.multiply(gate, down_grad.send(0))
    up_grad = PiecedGradient(low_all, both_all, y_first, 1)
    gate = up_grad.multiply(gate, down_grad.send(1))
    gate = last(per - 1, gate, down_grad.send(2), gate_grad.send(0))
    o_grad = Gradient(with_near(d_branch), with_near(att), z_first)
    gate = o_grad.multiply(gate)
    gates = [gate, gate_grad.send(1), down_grad.add(gate)]

    parts, sums, q_terms, k_terms = [], [], [], []
    for h in range(nh):
        grads_in = [d_outs[c][s] for s in range(n_ctx) for c in chunks]
        grads_in[0] = after(grads_in[0], *gates)
        back = attend_back(place, qkvs[h], grads_in, h, attended[h][0], attended[h][1], block)
        gates = [back[0]]
        if h == 0:
            arrived = [p for s, p in enumerate(d_outs[-1]) if s]
            gates += [up_grad.send(0, *arrived), up_grad.send(1, *arrived), gate_grad.send(2)]
        parts.append([back[0]] + [swap(back[s], "ctx", s) for s in range(1, n_ctx)])
    gates += [down_grad.send(0), down_grad.send(1), gate_grad.send(3)]
    for h in range(nh):
        mine = [after(parts[h][0], *gates)] + parts[h][1:]
        sum_h, q_term, k_term = back_sums(
            col, mine, query_raw, key_raw, q_scale, k_scale, qg, kg, cosine, sine, h
        )
        gates = [sum_h]
        sums.append(sum_h)
        q_terms.append(q_term)
        k_terms.append(k_term)
    gate_grad.add(sums[0])
    down_grad.add(sums[0])
    o_grad.step(sums[0])
    flat_parts = [part for mine in parts for part in mine]
    both = tensor_sum(sum(sums)) / features
    q_mean = both[0][:, None] * q_scale**3
    k_mean = both[1][:, None] * k_scale**3
    d_qkv, input_sums = [], []
    for c in chunks:
        d, part = back_prep(
            c, block, col, flat_parts, query_raw, key_raw, q_scale, k_scale, after(q_mean, *gates), k_mean,
            qg, kg, cosine, sine, q_weight, k_weight, v_weight, n_ctx, nh
        )
        gates = [part]
        d_qkv.append(d)
        input_sums.append(tensor_list(part))
    flat_near = near(flat)
    token_rows = [(t, c) for t in (flat, flat_near) for c in chunks]
    qkv_all = with_near(d_qkv)
    smalls = [Gradient(token_rows, qkv_all, y_first, i) for i in (2, 0, 1)]
    gates += [up_grad.send(2), up_grad.send(3)]
    for small in smalls:
        gates = [small.multiply(*gates)]
    up_grad.add(*gates)
    o_grad.step(*gates)
    done = [small.step(*gates) for small in smalls]
    done += [down_grad.add(*done), gate_grad.add(*done)]

    input_grad = []
    for c in chunks:
        terms = hid[c] + input_sums[c]
        terms[0] = after(terms[0], *gates)
        input_grad = [total_rows(c, cot, terms, input_grad)]

    results = [small.result() for small in smalls]
    gains = jnp.concatenate([sum(q_terms), sum(k_terms), sum(attn_terms), sum(mlp_terms)], axis=1)
    gains = after(gains.reshape(-1, 128), *gates, *done, input_grad[0])
    for axis, bit in y_first:
        gains = gains + swap(gains, axis, bit)
    gains = gains.reshape(-1)
    own = heads_here * HD

    return (
        output[0].reshape(local, seqs, width),
        input_grad[0].reshape(local, seqs, width),
        results[1],
        results[2],
        results[0],
        o_grad.result(),
        gate_grad.result(),
        up_grad.result(),
        down_grad.result(),
        gains[:own],
        gains[own : 2 * own],
        gains[2 * own : 2 * own + width],
        gains[2 * own + width :],
    )


def rounded(value):
    return lax.optimization_barrier(value.astype(jnp.bfloat16)).astype(jnp.float32)


def rotate(value, cosine, sine):
    half = value.shape[-1] // 2
    first = value[..., :half]
    second = value[..., half:]
    return jnp.concatenate(
        [first * cosine - second * sine, second * cosine + first * sine], axis=-1
    )


def unrotate(grad, cosine, sine):
    half = grad.shape[-1] // 2
    first = grad[..., :half]
    second = grad[..., half:]
    return jnp.concatenate(
        [first * cosine + second * sine, second * cosine - first * sine], axis=-1
    )


def position_table(group_order, length):
    groups = group_order.shape[1]
    block = length // groups
    slots = jnp.arange(length, dtype=jnp.int32)
    onehot = (slots // block)[:, None] == jnp.arange(groups, dtype=jnp.int32)[None, :]
    picked = jnp.sum(jnp.where(onehot[:, None, :], group_order[None, :, :], 0), axis=-1)
    return picked * block + (slots % block)[:, None]


def branch_total(term, total_rows):
    return lax.psum(term(0, total_rows).astype(jnp.bfloat16), "tensor").astype(jnp.float32)


def branch_gains(attn_term, mlp_term):
    return (attn_term, mlp_term)


def gathered_device(
    tokens,
    q_weight,
    k_weight,
    v_weight,
    o_weight,
    gate_weight,
    up_weight,
    down_weight,
    q_gain,
    k_gain,
    attn_gain,
    mlp_gain,
    group_order,
    cotangent,
):
    local, seqs, width = tokens.shape
    rows = local * seqs
    heads_here = q_weight.shape[1] // HD
    features = H * HD
    scale = HD ** (-0.5)
    flat = tokens.reshape(rows, width)
    query_raw = plain(flat, q_weight)
    key_raw = plain(flat, k_weight)
    value_raw = plain(flat, v_weight)
    square_sums = lax.psum(
        (jnp.sum(query_raw * query_raw, -1), jnp.sum(key_raw * key_raw, -1)), "tensor"
    )
    q_scale = lax.rsqrt(square_sums[0] / features + EPS)[:, None]
    k_scale = lax.rsqrt(square_sums[1] / features + EPS)[:, None]
    q_normed = query_raw * q_scale * q_gain
    k_normed = key_raw * k_scale * k_gain
    length = local * lax.axis_size("ctx")
    offset = lax.axis_index("ctx") * local
    positions = position_table(group_order, length)
    query_pos = lax.dynamic_slice_in_dim(positions, offset, local, 0)
    freq = jnp.power(THETA, -jnp.arange(HD // 2, dtype=jnp.float32) * 2.0 / HD)
    angle = query_pos.astype(jnp.float32)[..., None] * freq
    cosine = jnp.cos(angle)[:, :, None, :]
    sine = jnp.sin(angle)[:, :, None, :]
    queries = rotate(q_normed.reshape(local, seqs, heads_here, HD), cosine, sine).astype(
        jnp.bfloat16
    )
    keys = rotate(k_normed.reshape(local, seqs, heads_here, HD), cosine, sine).astype(jnp.bfloat16)
    values = value_raw.reshape(local, seqs, heads_here, HD).astype(jnp.bfloat16)
    query_side = jnp.transpose(query_pos)

    def allowed_mask():
        key_pos = jnp.transpose(positions)
        return key_pos[:, None, None, :] <= query_side[:, None, :, None]

    top = jnp.full((seqs, heads_here, local), -1e30, jnp.float32)
    keys_in = lax.all_gather(keys, "ctx", axis=0, tiled=True)
    values_in = lax.all_gather(values, "ctx", axis=0, tiled=True)
    allowed = allowed_mask()
    scores = (
        jnp.einsum("qshd,kshd->shqk", queries, keys_in, preferred_element_type=jnp.float32) * scale
    )
    scores = jnp.where(allowed, scores, -1e30)
    new_top = jnp.maximum(top, jnp.max(scores, axis=-1))
    expo = jnp.where(allowed, jnp.exp(scores - new_top[..., None]), 0.0)
    total = jnp.sum(expo, axis=-1)
    product = jnp.einsum(
        "shqk,kshd->qshd", expo.astype(jnp.bfloat16), values_in, preferred_element_type=jnp.float32
    )
    accum = product
    top, total, accum = (new_top, total, accum)
    log_total = top + jnp.log(total)
    attended = accum / jnp.transpose(total, (2, 0, 1))[..., None]
    attended_low = attended.reshape(rows, heads_here * HD).astype(jnp.bfloat16)

    def attention_term(start, count):
        return times_trans(attended_low, o_weight)

    branch = branch_total(attention_term, rows)
    a_scale = lax.rsqrt(jnp.mean(branch * branch, axis=-1, keepdims=True) + EPS)
    hidden = flat.astype(jnp.float32) + branch * a_scale * attn_gain
    lowered = hidden.astype(jnp.bfloat16)
    gate = plain(lowered, gate_weight)
    up = plain(lowered, up_weight)
    sigmoid = jax.nn.sigmoid(gate)
    silu_gate = gate * sigmoid
    inner = (silu_gate * up).astype(jnp.bfloat16)

    def mixer_term(start, count):
        return times_trans(inner, down_weight)

    mixed = branch_total(mixer_term, rows)
    m_scale = lax.rsqrt(jnp.mean(mixed * mixed, axis=-1, keepdims=True) + EPS)
    output = hidden + mixed * m_scale * mlp_gain
    output_low = output.astype(jnp.bfloat16)
    grad = cotangent.reshape(rows, width).astype(jnp.float32)
    mlp_gain_term = jnp.sum(grad * mixed * m_scale, axis=0)
    weighted = grad * mlp_gain
    d_mixed_own = (
        m_scale * weighted - mixed * m_scale**3 * jnp.mean(weighted * mixed, axis=-1, keepdims=True)
    ).astype(jnp.bfloat16)
    down_grad = row_dot(d_mixed_own, inner)
    d_inner = plain(d_mixed_own, down_weight)
    d_gate = (d_inner * up * (sigmoid + silu_gate * (1.0 - sigmoid))).astype(jnp.bfloat16)
    d_up = (d_inner * silu_gate).astype(jnp.bfloat16)
    gate_grad = row_dot(lowered, d_gate)
    up_grad = row_dot(lowered, d_up)

    def mixer_back_term(start, count):
        return times_trans(d_gate, gate_weight) + times_trans(d_up, up_weight)

    d_hidden = grad + branch_total(mixer_back_term, rows)
    attn_gain_term = jnp.sum(d_hidden * branch * a_scale, axis=0)
    weighted = d_hidden * attn_gain
    d_branch_own = (
        a_scale * weighted
        - branch * a_scale**3 * jnp.mean(weighted * branch, axis=-1, keepdims=True)
    ).astype(jnp.bfloat16)
    o_grad = row_dot(d_branch_own, attended_low)
    d_attended = (
        plain(d_branch_own, o_weight).astype(jnp.bfloat16).reshape(local, seqs, heads_here, HD)
    )
    delta = jnp.transpose(jnp.sum(d_attended.astype(jnp.float32) * attended, axis=-1), (1, 2, 0))
    keys_in = lax.all_gather(keys, "ctx", axis=0, tiled=True)
    values_in = lax.all_gather(values, "ctx", axis=0, tiled=True)
    allowed = allowed_mask()
    scores = (
        jnp.einsum("qshd,kshd->shqk", queries, keys_in, preferred_element_type=jnp.float32) * scale
    )
    weights = jnp.where(allowed, jnp.exp(scores - log_total[..., None]), 0.0)
    d_vals = jnp.einsum(
        "shqk,qshd->kshd",
        weights.astype(jnp.bfloat16),
        d_attended,
        preferred_element_type=jnp.float32,
    )
    d_weights = jnp.einsum(
        "qshd,kshd->shqk", d_attended, values_in, preferred_element_type=jnp.float32
    )
    d_scores = (weights * (d_weights - delta[..., None])).astype(jnp.bfloat16)
    d_query_sum = (
        jnp.einsum("shqk,kshd->qshd", d_scores, keys_in, preferred_element_type=jnp.float32) * scale
    )
    d_keys_part = (
        jnp.einsum("shqk,qshd->kshd", d_scores, queries, preferred_element_type=jnp.float32) * scale
    )
    update = jnp.stack([d_keys_part, d_vals], axis=2)
    grad_table = update
    d_query_sum, grad_table = (d_query_sum, grad_table)
    own_grads = lax.psum_scatter(
        grad_table.astype(jnp.bfloat16), "ctx", scatter_dimension=0, tiled=True
    ).astype(jnp.float32)
    d_qnorm = unrotate(rounded(d_query_sum), cosine, sine).reshape(rows, heads_here * HD)
    d_knorm = unrotate(rounded(own_grads[:, :, 0]), cosine, sine).reshape(rows, heads_here * HD)
    d_value = own_grads[:, :, 1].astype(jnp.bfloat16).reshape(rows, heads_here * HD)
    q_gain_term = jnp.sum(d_qnorm * query_raw * q_scale, axis=0)
    k_gain_term = jnp.sum(d_knorm * key_raw * k_scale, axis=0)
    q_weighted = d_qnorm * q_gain
    k_weighted = d_knorm * k_gain
    back_sums = lax.psum(
        (jnp.sum(q_weighted * query_raw, -1), jnp.sum(k_weighted * key_raw, -1)), "tensor"
    )
    d_qraw = (
        q_scale * q_weighted - query_raw * q_scale**3 * (back_sums[0] / features)[:, None]
    ).astype(jnp.bfloat16)
    d_kraw = (
        k_scale * k_weighted - key_raw * k_scale**3 * (back_sums[1] / features)[:, None]
    ).astype(jnp.bfloat16)
    q_grad = row_dot(flat, d_qraw)
    k_grad = row_dot(flat, d_kraw)
    v_grad = row_dot(flat, d_value)

    def input_term(start, count):
        total_part = times_trans(d_qraw, q_weight)
        total_part = total_part + times_trans(d_kraw, k_weight)
        return total_part + times_trans(d_value, v_weight)

    d_input = d_hidden + branch_total(input_term, rows)
    input_low = d_input.astype(jnp.bfloat16)
    totals = (
        lax.psum_scatter(
            q_grad.astype(jnp.bfloat16), ("dp", "ctx"), scatter_dimension=0, tiled=True
        ).astype(jnp.float32),
        lax.psum_scatter(
            k_grad.astype(jnp.bfloat16), ("dp", "ctx"), scatter_dimension=0, tiled=True
        ).astype(jnp.float32),
        lax.psum_scatter(
            v_grad.astype(jnp.bfloat16), ("dp", "ctx"), scatter_dimension=0, tiled=True
        ).astype(jnp.float32),
        lax.psum_scatter(
            o_grad.astype(jnp.bfloat16), ("dp", "ctx"), scatter_dimension=0, tiled=True
        ).astype(jnp.float32),
        lax.psum_scatter(
            gate_grad.astype(jnp.bfloat16), ("dp", "ctx"), scatter_dimension=0, tiled=True
        ).astype(jnp.float32),
        lax.psum_scatter(
            up_grad.astype(jnp.bfloat16), ("dp", "ctx"), scatter_dimension=0, tiled=True
        ).astype(jnp.float32),
        lax.psum_scatter(
            down_grad.astype(jnp.bfloat16), ("dp", "ctx"), scatter_dimension=0, tiled=True
        ).astype(jnp.float32),
    )
    attn_gain_part, mlp_gain_part = branch_gains(attn_gain_term, mlp_gain_term)
    gain_totals = lax.psum((q_gain_term, k_gain_term, attn_gain_part, mlp_gain_part), ("dp", "ctx"))
    output_out = output_low.reshape(local, seqs, width)
    input_out = input_low.reshape(local, seqs, width)
    return (
        output_out,
        input_out,
        totals[0],
        totals[1],
        totals[2],
        totals[3],
        totals[4],
        totals[5],
        totals[6],
        gain_totals[0],
        gain_totals[1],
        gain_totals[2],
        gain_totals[3],
    )


def solution(mesh):
    in_specs = (
        P("ctx", "dp", None),
        P(None, "tensor"),
        P(None, "tensor"),
        P(None, "tensor"),
        P(None, "tensor"),
        P(None, "tensor"),
        P(None, "tensor"),
        P(None, "tensor"),
        P("tensor"),
        P("tensor"),
        P(),
        P(),
        P("dp", None),
        P("ctx", "dp", None),
    )
    out_specs = (
        P("ctx", "dp", None),
        P("ctx", "dp", None),
        P(("dp", "ctx"), "tensor"),
        P(("dp", "ctx"), "tensor"),
        P(("dp", "ctx"), "tensor"),
        P(("dp", "ctx"), "tensor"),
        P(("dp", "ctx"), "tensor"),
        P(("dp", "ctx"), "tensor"),
        P(("dp", "ctx"), "tensor"),
        P("tensor"),
        P("tensor"),
        P(),
        P(),
    )
    heads_here = H // mesh.shape["tensor"]
    whole_heads = heads_here % mesh.shape["ctx"] == 0
    return jax.shard_map(
        on_device if whole_heads else gathered_device, mesh=mesh, in_specs=in_specs, out_specs=out_specs, check_vma=False
    )
```
